32 devices in a mesh: rep: 8 (over z, x), shard: 4 (over y, core).
Axes of the slice: x: 2, y: 2, z: 4, core: 2. Of those that a mesh axis runs over, the one named last changes fastest.
Arguments:
- grads: bfloat16 [8, 4, 512, 3968], P('rep', 'shard'), may hold values from -6 to 6
- error: float32 [8, 512, 3968], P('rep', 'shard'), may hold values from -6 to 6
- q_factor: float32 [32, 3968], replicated, may hold values from -0.09375 to 0.09375
Outputs:
- approx: float32 [512, 3968], P('shard')
- new_error: float32 [8, 512, 3968], P('rep', 'shard')
- q_next: float32 [32, 3968], replicated
The draws below stay inside these ranges and needn't reach their ends.
All inputs are finite; a program needn't handle non-finite values.
Results may differ from the reference program's by a relative error of at most 0.0003.
Values sent between devices are 32-bit elements; how exact they have to be, the bound alone decides.
No kernel may reach another device: no remote copies, remote signals or barrier semaphores. Data moves between devices by JAX's collectives and lax.ppermute only.
A program may use at most 128 MiB of HBM per device.

```python
import jax
import jax.numpy as jnp
from jax import lax

COLS = 3968
RANK = 32
ROWS = 512
N_REP = 8
N_SHARD = 4


def with_spikes(values, key, source, target, blocks, factor):
    owner, partner = [(jnp.arange(values.shape[axis_at]) // (values.shape[axis_at] // blocks)).reshape([-1 if axis == axis_at else 1 for axis in range(values.ndim)]) for axis_at in (source, target)]
    chosen = jax.random.permutation(key, blocks)[partner]
    strong = (owner == chosen) | (owner == (partner + blocks // 2) % blocks)
    return jnp.where(strong, factor * values, values)


def levels(rng, dims, shards, smallest, largest):
    loudness, own = 1.0, jax.random.fold_in(rng, 6)
    for position, blocks in shards:
        draws = jnp.exp(jax.random.uniform(jax.random.fold_in(own, position), (blocks,), jnp.float32, smallest / len(shards), largest / len(shards)))
        loudness = loudness * jnp.repeat(draws, dims[position] // blocks).reshape([-1 if axis == position else 1 for axis in range(len(dims))])
    return loudness


def centred(own_key, extent, spread, limit, split=(), dtype=jnp.bfloat16):
    array = spread * jax.random.normal(own_key, extent, jnp.float32)
    if split:
        array = array * levels(own_key, extent, split, -0.22, 0.18)
    return jnp.clip(array, -limit, limit).astype(dtype)


def noise_with(stream_key, shape, scale, bound, pieces, heavy, held_as=jnp.bfloat16):
    array = scale * jax.random.normal(stream_key, shape, jnp.float32)
    if pieces:
        array = array * levels(stream_key, shape, pieces, -0.22, 0.18)
    return jnp.clip(with_spikes(array, jax.random.fold_in(stream_key, 3), *heavy), -bound, bound).astype(held_as)


def setup_inputs(seed: int = 0) -> dict:
    streams_of = jax.random.split(jax.random.key(seed), 4)
    grads = noise_with(streams_of[0], (N_REP, N_SHARD, ROWS, COLS), 1.0, 6.0, ((0, 8), (1, 4)), (1, 2, 4, 2.0))
    error = centred(streams_of[1], (N_REP, ROWS, COLS), 1.0, 6.0, ((0, 8), (1, 4)), jnp.float32)
    q_factor = centred(streams_of[2], (RANK, COLS), COLS ** -0.5, 0.09375, (), jnp.float32)
    return {"grads": grads, "error": error, "q_factor": q_factor}


def merge_rows(grad_terms, error_rows):
    return jnp.sum(grad_terms.astype(jnp.float32), axis=0) + error_rows

def reference(grads, error, q_factor):

    def left_term(pair):
        merged = merge_rows(pair[0], pair[1])
        return jnp.dot(merged.astype(jnp.float32), q_factor.T.astype(jnp.float32), precision=lax.Precision.HIGHEST, preferred_element_type=jnp.float32)
    factor = jnp.sum(lax.map(left_term, (grads, error)), axis=0)
    gram = jnp.dot(factor.T.astype(jnp.float32), factor.astype(jnp.float32), precision=lax.Precision.HIGHEST, preferred_element_type=jnp.float32)
    lower = jnp.linalg.cholesky(gram)
    basis_t = jax.scipy.linalg.solve_triangular(lower, factor.T, lower=True)

    def right_term(pair):
        merged = merge_rows(pair[0], pair[1])
        return jnp.dot(basis_t.astype(jnp.float32), merged.astype(jnp.float32), precision=lax.Precision.HIGHEST, preferred_element_type=jnp.float32)
    q_next = jnp.sum(lax.map(right_term, (grads, error)), axis=0) / N_REP
    approx = jnp.dot(basis_t.T.astype(jnp.float32), q_next.astype(jnp.float32), precision=lax.Precision.HIGHEST, preferred_element_type=jnp.float32)

    def error_term(pair):
        return merge_rows(pair[0], pair[1]) - approx
    new_error = lax.map(error_term, (grads, error))
    return (approx, new_error, q_next)
```

```python
import functools

import jax
import jax.numpy as jnp
from jax import lax
from jax.experimental import pallas as pl
from jax.experimental.pallas import tpu as pltpu
from jax.sharding import PartitionSpec as P

F32 = jnp.float32
BF16 = jnp.bfloat16
LANES = 128
WIDE = 512
VMEM_LIMIT = 48 * 1024 * 1024


def pieces(x):
    high = x.astype(BF16)
    rest = x - high.astype(F32)
    mid = rest.astype(BF16)
    low = (rest - mid.astype(F32)).astype(BF16)
    return jnp.concatenate([high, mid, low], axis=0)


def fold(x, rank):
    return (x[2 * rank :] + x[rank : 2 * rank]) + x[:rank]


def dot(a, b, contract, precision=None):
    return lax.dot_general(
        a, b, (contract, ((), ())), precision=precision, preferred_element_type=F32
    )


def tree(values):
    values = list(values)
    while len(values) > 1:
        values = [values[i] + values[i + 1] for i in range(0, len(values), 2)]
    return values[0]


def params(**kw):
    return pltpu.CompilerParams(vmem_limit_bytes=VMEM_LIMIT, **kw)


def cost(flops, moved):
    return pl.CostEstimate(flops=int(flops), bytes_accessed=int(moved), transcendentals=0)


def partner(x, axis, d):
    n = lax.axis_size(axis)
    return lax.ppermute(x, axis, [(i, i ^ d) for i in range(n)])


def whole(shape):
    return pl.BlockSpec(shape, lambda *_: (0,) * len(shape))


def widen(where, grads, block_rows, first, count):
    step = 16
    cols = grads.shape[1]

    def kernel(where_ref, g_ref, o_ref):
        o_ref[...] = g_ref[...].astype(F32)

    return pl.pallas_call(
        kernel,
        out_shape=jax.ShapeDtypeStruct((count, cols), F32),
        grid_spec=pltpu.PrefetchScalarGridSpec(
            num_scalar_prefetch=1,
            grid=(count // step,),
            in_specs=[
                pl.BlockSpec(
                    (step, cols), lambda i, w: (w[0] * (block_rows // step) + first // step + i, 0)
                )
            ],
            out_specs=pl.BlockSpec((step, cols), lambda i, w: (i, 0)),
        ),
        compiler_params=params(),
        cost_estimate=cost(count * cols, 6 * count * cols),
        name="widen_rows",
    )(where, grads)


def add_rows(where, grads, arrived, block_rows, first):
    step = 16
    count, cols = arrived.shape

    def kernel(where_ref, g_ref, a_ref, o_ref):
        o_ref[...] = g_ref[...].astype(F32) + a_ref[...]

    return pl.pallas_call(
        kernel,
        out_shape=jax.ShapeDtypeStruct((count, cols), F32),
        grid_spec=pltpu.PrefetchScalarGridSpec(
            num_scalar_prefetch=1,
            grid=(count // step,),
            in_specs=[
                pl.BlockSpec(
                    (step, cols), lambda i, w: (w[0] * (block_rows // step) + first // step + i, 0)
                ),
                pl.BlockSpec((step, cols), lambda i, w: (i, 0)),
            ],
            out_specs=pl.BlockSpec((step, cols), lambda i, w: (i, 0)),
        ),
        compiler_params=params(),
        cost_estimate=cost(count * cols, 10 * count * cols),
        name="add_rows",
    )(where, grads, arrived)


def left_terms(me, grads, q_factor, n_shard):
    rows, cols = grads.shape
    block = rows // n_shard
    rank = q_factor.shape[0]

    def kernel(me_ref, g_ref, q_ref, *rest):
        outs, wide_ref, q3 = rest[:n_shard], rest[n_shard], rest[n_shard + 1]
        i = pl.program_id(0)

        @pl.when(i == 0)
        def _():
            q3[...] = pieces(q_ref[...])

        g = g_ref[...]
        term = fold(dot(q3[...], g, ((1,), (1,))), rank)
        for d in range(n_shard):

            @pl.when(i == n_shard - 1 - d)
            def _(d=d):
                outs[d][...] = term

        @pl.when(i == n_shard - 2)
        def _():
            wide_ref[...] = g.astype(F32)

    return pl.pallas_call(
        kernel,
        out_shape=[jax.ShapeDtypeStruct((rank, block), F32)] * n_shard
        + [jax.ShapeDtypeStruct((block, cols), F32)],
        grid_spec=pltpu.PrefetchScalarGridSpec(
            num_scalar_prefetch=1,
            grid=(n_shard,),
            in_specs=[
                pl.BlockSpec((block, cols), lambda i, w: (w[0] ^ (n_shard - 1 - i), 0)),
                whole((rank, cols)),
            ],
            out_specs=[whole((rank, block))] * n_shard + [whole((block, cols))],
            scratch_shapes=[pltpu.VMEM((3 * rank, cols), BF16)],
        ),
        compiler_params=params(),
        cost_estimate=cost(6 * rank * rows * cols, 2 * rows * cols + 4 * block * cols),
        name="left_terms",
    )(me, grads, q_factor)


def error_term(error, q_factor, term):
    rows, cols = error.shape
    rank = q_factor.shape[0]

    def kernel(e_ref, q_ref, t_ref, o_ref):
        q3 = pieces(q_ref[...])
        e3 = pieces(e_ref[...])
        high, mid, low = e3[:rows], e3[rows : 2 * rows], e3[2 * rows :]
        nt = ((1,), (1,))
        a = fold(dot(q3, high, nt), rank)
        b = dot(q3[: 2 * rank], mid, nt)
        c = dot(q3[:rank], low, nt)
        o_ref[...] = t_ref[...] + (a + ((b[:rank] + b[rank:]) + c))

    return pl.pallas_call(
        kernel,
        out_shape=jax.ShapeDtypeStruct((rank, rows), F32),
        compiler_params=params(),
        cost_estimate=cost(12 * rank * rows * cols, 4 * rows * cols),
        name="error_term",
    )(error, q_factor, term)


def total(*values):
    def kernel(*refs):
        refs[-1][...] = tree([r[...] for r in refs[:-1]])

    return pl.pallas_call(
        kernel,
        out_shape=jax.ShapeDtypeStruct(values[0].shape, F32),
        compiler_params=params(),
        cost_estimate=cost(0, 4 * values[0].size),
        name="total",
    )(*values)


def right_terms(me, grads, error, blocks, n_shard):
    rows, cols = grads.shape
    block = rows // n_shard
    rank = blocks[0].shape[0]
    per = WIDE // LANES
    n_wide = 2 * (-(-cols // (2 * WIDE)))
    half = n_wide // 2
    out = jax.ShapeDtypeStruct((half * per * rank, LANES), F32)

    def kernel(me_ref, g_ref, e_ref, *rest):
        b_refs = rest[:n_shard]
        send_ref, keep_ref, f_all, f3 = rest[n_shard:]
        i = pl.program_id(0)

        @pl.when(i == 0)
        def _():
            for d in range(n_shard):
                f_all[me_ref[0] ^ d] = b_refs[d][...]
            f3[...] = pieces(jnp.concatenate([f_all[j] for j in range(n_shard)], axis=1))

        value = fold(dot(f3[...], g_ref[...], ((1,), (0,))), rank)
        value += dot(b_refs[0][...], e_ref[...], ((1,), (0,)), lax.Precision.HIGHEST)
        stacked = jnp.concatenate(
            [value[:, k * LANES : (k + 1) * LANES] for k in range(per)], axis=0
        )

        @pl.when(i < half)
        def _():
            send_ref[...] = stacked

        @pl.when(i >= half)
        def _():
            keep_ref[...] = stacked

    def col(i, w):
        return (i + half * (1 - (w[0] & 1))) % n_wide

    return pl.pallas_call(
        kernel,
        out_shape=[out, out],
        grid_spec=pltpu.PrefetchScalarGridSpec(
            num_scalar_prefetch=1,
            grid=(n_wide,),
            in_specs=[
                pl.BlockSpec((rows, WIDE), lambda i, w: (0, col(i, w))),
                pl.BlockSpec((block, WIDE), lambda i, w: (0, col(i, w))),
            ]
            + [whole((rank, block))] * n_shard,
            out_specs=[
                pl.BlockSpec((per * rank, LANES), lambda i, w: (jnp.minimum(i, half - 1), 0)),
                pl.BlockSpec((per * rank, LANES), lambda i, w: (jnp.maximum(i - half, 0), 0)),
            ],
            scratch_shapes=[
                pltpu.VMEM((n_shard, rank, block), F32),
                pltpu.VMEM((3 * rank, rows), BF16),
            ],
        ),
        compiler_params=params(),
        cost_estimate=cost(6 * rank * rows * cols, 2 * rows * cols + 4 * block * cols),
        name="right_terms",
    )(me, grads, error, *blocks)


def inverse_factor(me, blocks, n_shard):
    rank, block = blocks[0].shape

    def kernel(me_ref, *rest):
        b_refs = rest[:n_shard]
        inv_ref, basis_ref, f_all = rest[n_shard:]
        for d in range(n_shard):
            f_all[me_ref[0] ^ d] = b_refs[d][...]
        f = jnp.concatenate([f_all[j] for j in range(n_shard)], axis=1)
        gram = dot(f, f, ((1,), (1,)), lax.Precision.HIGHEST)
        row = lax.broadcasted_iota(jnp.int32, (rank, 2 * rank), 0)
        col = lax.broadcasted_iota(jnp.int32, (rank, 2 * rank), 1)
        unit = jnp.where(col == row + rank, 1.0, 0.0).astype(F32)
        w = jnp.concatenate([gram, jnp.zeros_like(gram)], axis=1) + unit
        for k in range(rank):
            scale = 1.0 / jnp.sqrt(w[k : k + 1, k : k + 1])
            pivot = w[k : k + 1, :] * scale
            column = w[:, k : k + 1] * scale
            w = jnp.where(row > k, w - column * pivot, jnp.where(row == k, pivot, w))
        inverse = w[:, rank:]
        inv_ref[...] = inverse
        basis_ref[...] = dot(inverse, b_refs[0][...], ((1,), (0,)), lax.Precision.HIGHEST)

    vmem = pl.BlockSpec(memory_space=pltpu.VMEM)
    return pl.pallas_call(
        kernel,
        out_shape=[
            jax.ShapeDtypeStruct((rank, rank), F32),
            jax.ShapeDtypeStruct((rank, block), F32),
        ],
        in_specs=[pl.BlockSpec(memory_space=pltpu.SMEM)] + [vmem] * n_shard,
        out_specs=[vmem, vmem],
        scratch_shapes=[pltpu.VMEM((n_shard, rank, block), F32)],
        compiler_params=params(),
        cost_estimate=cost(rank**3 * 100, 8 * rank * block),
        name="inverse_factor",
    )(me, *blocks)


def split_sum(own, keep, arrived, n_rep):
    rows = keep.shape[0] // n_rep

    def kernel(own_ref, k_ref, a_ref, *outs):
        for d in range(n_rep):
            at = pl.ds(pl.multiple_of((own_ref[0] ^ d) * rows, rows), rows)
            outs[d][...] = k_ref[at, :] + a_ref[at, :]

    vmem = pl.BlockSpec(memory_space=pltpu.VMEM)
    return pl.pallas_call(
        kernel,
        out_shape=[jax.ShapeDtypeStruct((rows, LANES), F32)] * n_rep,
        in_specs=[pl.BlockSpec(memory_space=pltpu.SMEM), vmem, vmem],
        out_specs=[vmem] * n_rep,
        compiler_params=params(),
        cost_estimate=cost(keep.size, 12 * keep.size),
        name="split_sum",
    )(own, keep, arrived)


def join(own, parts):
    n = len(parts)
    rows = parts[0].shape[0]

    def kernel(own_ref, *refs):
        for d in range(n):
            at = pl.ds(pl.multiple_of((own_ref[0] ^ d) * rows, rows), rows)
            refs[n][at, :] = refs[d][...]

    vmem = pl.BlockSpec(memory_space=pltpu.VMEM)
    return pl.pallas_call(
        kernel,
        out_shape=jax.ShapeDtypeStruct((n * rows, LANES), F32),
        in_specs=[pl.BlockSpec(memory_space=pltpu.SMEM)] + [vmem] * n,
        out_specs=vmem,
        compiler_params=params(),
        cost_estimate=cost(0, 8 * n * rows * LANES),
        name="join",
    )(own, *parts)


def own_rows(me, grads, arrived, error, block_rows):
    step = 32
    count, cols = error.shape

    def kernel(me_ref, g_ref, a_ref, e_ref, o_ref):
        o_ref[...] = (g_ref[...].astype(F32) + a_ref[...]) + e_ref[...]

    rowwise = pl.BlockSpec((step, cols), lambda i, w: (i, 0))
    return pl.pallas_call(
        kernel,
        out_shape=jax.ShapeDtypeStruct((count, cols), F32),
        grid_spec=pltpu.PrefetchScalarGridSpec(
            num_scalar_prefetch=1,
            grid=(count // step,),
            in_specs=[
                pl.BlockSpec((step, cols), lambda i, w: (w[0] * (block_rows // step) + i, 0)),
                rowwise,
                rowwise,
            ],
            out_specs=rowwise,
        ),
        compiler_params=params(),
        cost_estimate=cost(2 * count * cols, 14 * count * cols),
        name="own_rows",
    )(me, grads, arrived, error)


def finish(core, inverse, basis, q_own, q_other, partial, arrived, n_rep):
    rows, cols = partial.shape
    rank = inverse.shape[0]
    per = WIDE // LANES
    n_wide = -(-cols // WIDE)
    half = q_own.shape[0] // (per * rank)
    counts = [a.shape[0] for a in arrived]
    n_arrived = len(arrived)

    def kernel(core_ref, inv_ref, basis_ref, own_ref, other_ref, p_ref, *rest):
        a_refs = rest[:n_arrived]
        approx_ref, error_ref, q_ref = rest[n_arrived:]
        j = pl.program_id(0)
        mine = (j // half) == core_ref[0]
        stacked = jnp.where(mine, own_ref[...], other_ref[...])
        q_sum = jnp.concatenate(
            [stacked[k * rank : (k + 1) * rank] for k in range(per)], axis=1
        )
        q_next = dot(inv_ref[...], q_sum, ((1,), (0,)), lax.Precision.HIGHEST) * (1.0 / n_rep)
        q_ref[...] = q_next
        approx = dot(basis_ref[...], q_next, ((0,), (0,)), lax.Precision.HIGHEST)
        approx_ref[...] = approx
        merged = p_ref[...]
        values = jnp.concatenate([a_ref[...] for a_ref in a_refs], axis=0)
        error_ref[...] = (merged + values) - approx

    wide = lambda r: pl.BlockSpec((r, WIDE), lambda j, c: (0, j))
    q_spec = pl.BlockSpec((per * rank, LANES), lambda j, c: (j % half, 0))
    return pl.pallas_call(
        kernel,
        out_shape=[
            jax.ShapeDtypeStruct((rows, cols), F32),
            jax.ShapeDtypeStruct((rows, cols), F32),
            jax.ShapeDtypeStruct((rank, cols), F32),
        ],
        grid_spec=pltpu.PrefetchScalarGridSpec(
            num_scalar_prefetch=1,
            grid=(n_wide,),
            in_specs=[whole(inverse.shape), whole(basis.shape), q_spec, q_spec, wide(rows)]
            + [wide(count) for count in counts],
            out_specs=[wide(rows), wide(rows), wide(rank)],
        ),
        compiler_params=params(),
        cost_estimate=cost(12 * rank * rows * cols, 16 * rows * cols),
        name="finish",
    )(core, inverse, basis, q_own, q_other, partial, *arrived)


def body(grads, error, q_factor):
    n_rep, n_shard = lax.axis_size("rep"), lax.axis_size("shard")
    grads, error = grads[0, 0], error[0]
    rows, cols = grads.shape
    block = rows // n_shard
    rank = q_factor.shape[0]
    me = lax.axis_index("shard").astype(jnp.int32)
    own = lax.axis_index("rep").astype(jnp.int32).reshape(1)
    core = (me & 1).reshape(1)
    me = me.reshape(1)

    cuts = ((0, 32), (32, 48), (80, 48))
    crossing = [[] for _ in cuts]
    for d in range(2, n_shard, 2):
        for k, (first, count) in enumerate(cuts):
            to_core = widen(me ^ (d + 1), grads, block, first, count)
            to_core = partner(to_core, "shard", 1)
            to_chip = add_rows(me ^ d, grads, to_core, block, first)
            crossing[k].append(partner(to_chip, "shard", d))
    arrived = [parts[0] if len(parts) == 1 else sum(parts) for parts in crossing]

    *terms, to_core = left_terms(me, grads, q_factor, n_shard)
    from_core = partner(to_core, "shard", 1)
    received = [partner(terms[d], "shard", d) for d in range(1, n_shard)]
    factor_part = total(error_term(error, q_factor, terms[0]), *received)
    factor_own = total(
        factor_part, *[partner(factor_part, "rep", d) for d in range(1, n_rep)]
    )
    blocks = [factor_own] + [partner(factor_own, "shard", d) for d in range(1, n_shard)]

    send, keep = right_terms(me, grads, error, blocks, n_shard)
    cut = split_sum(own, keep, partner(send, "shard", 1), n_rep)
    piece = total(cut[0], *[partner(cut[d], "rep", d) for d in range(1, n_rep)])
    piece = total(piece, *[partner(piece, "shard", d) for d in range(2, n_shard, 2)])
    q_own = join(own, [piece] + [partner(piece, "rep", d) for d in range(1, n_rep)])
    q_other = partner(q_own, "shard", 1)

    inverse, basis = inverse_factor(me, blocks, n_shard)
    partial = own_rows(me, grads, from_core, error, block)
    approx, new_error, q_next = finish(
        core, inverse, basis, q_own, q_other, partial, arrived, n_rep
    )
    return approx, new_error[None], q_next


def solution(mesh):
    in_specs = (P("rep", "shard", None, None), P("rep", "shard", None), P())
    out_specs = (P("shard", None), P("rep", "shard", None), P())
    return jax.shard_map(body, mesh=mesh, in_specs=in_specs, out_specs=out_specs, check_vma=False)
```

```python
import jax
import jax.numpy as jnp
from jax import lax
from jax.experimental import pallas as pl
from jax.experimental.pallas import tpu as pltpu
from jax.sharding import Mesh, PartitionSpec as P

F32 = jnp.float32
BF16 = jnp.bfloat16
LANES = 128
WIDE = 512
VMEM_LIMIT = 24 * 1024 * 1024


def pieces(x):
    high = x.astype(BF16)
    rest = x - high.astype(F32)
    mid = rest.astype(BF16)
    low = (rest - mid.astype(F32)).astype(BF16)
    return jnp.concatenate([high, mid, low], axis=0)


def fold(x, rank):
    return (x[2 * rank :] + x[rank : 2 * rank]) + x[:rank]


def dot(a, b, contract, precision=None):
    return lax.dot_general(
        a, b, (contract, ((), ())), precision=precision, preferred_element_type=F32
    )


def six(x, axis, left):
    high = x.astype(BF16)
    rest = x - high.astype(F32)
    mid = rest.astype(BF16)
    low = (rest - mid.astype(F32)).astype(BF16)
    order = [high, high, mid, high, low, mid] if left else [high, mid, high, low, high, mid]
    return jnp.concatenate(order, axis=axis)


def params(limit=VMEM_LIMIT):
    return pltpu.CompilerParams(vmem_limit_bytes=limit)


NO_COST = pl.CostEstimate(flops=0, bytes_accessed=0, transcendentals=0)


def partner(x, axis, d):
    return lax.ppermute(x, axis, [(i, i ^ d) for i in range(lax.axis_size(axis))])


def whole(shape):
    return pl.BlockSpec(shape, lambda *_: (0,) * len(shape))


ANYWHERE = pl.BlockSpec(memory_space=pl.ANY)
VMEM = pl.BlockSpec(memory_space=pltpu.VMEM)
SMEM = pl.BlockSpec(memory_space=pltpu.SMEM)
HBM = pl.BlockSpec(memory_space=pltpu.HBM)


def exchange(parts, axes):
    return lax.all_to_all(parts, axes, split_axis=0, concat_axis=0, tiled=True)


def tree(values):
    values = list(values)
    while len(values) > 1:
        values = [sum(values[i + 1 : i + 2], values[i]) for i in range(0, len(values), 2)]
    return values[0]


def total(values, after=(), repeat=None):
    n = len(values)
    shape = values[0].shape

    def kernel(*refs):
        value = tree([r[...] for r in refs[:n]])
        if repeat is None:
            refs[-1][...] = value
        else:
            for k in range(repeat):
                refs[-1][k] = value

    return pl.pallas_call(
        kernel,
        out_shape=jax.ShapeDtypeStruct(shape if repeat is None else (repeat, *shape), F32),
        in_specs=[VMEM] * n + [ANYWHERE] * len(after),
        out_specs=VMEM,
        compiler_params=params(),
        cost_estimate=NO_COST,
        name="total",
    )(*values, *after)


def sum_parts(parts, after=()):
    n = parts.shape[0]

    def kernel(p_ref, *rest):
        rest[-1][...] = tree([p_ref[k] for k in range(n)])

    return pl.pallas_call(
        kernel,
        out_shape=jax.ShapeDtypeStruct(parts.shape[1:], F32),
        in_specs=[VMEM] + [ANYWHERE] * len(after),
        out_specs=VMEM,
        compiler_params=params(),
        cost_estimate=NO_COST,
        name="sum_parts",
    )(parts, *after)


def passed_on(value, after):
    def kernel(*refs):
        pass

    return pl.pallas_call(
        kernel,
        out_shape=jax.ShapeDtypeStruct(value.shape, value.dtype),
        in_specs=[ANYWHERE] * (1 + len(after)),
        out_specs=ANYWHERE,
        input_output_aliases={0: 0},
        compiler_params=params(),
        cost_estimate=NO_COST,
        name="passed_on",
    )(value, *after)


def join(me_ref, own_ref, other_ref, f_all):
    n_shard, rank, _ = f_all.shape
    half = n_shard // 2
    core = me_ref[0] & 1
    for k in range(half):
        f_all[2 * k + core] = own_ref[k * rank : (k + 1) * rank]
        f_all[2 * k + 1 - core] = other_ref[k * rank : (k + 1) * rank]


def spans(size, step):
    return [(at, min(step, size - at)) for at in range(0, size, step)]


def started(source, target, sem):
    copy = pltpu.make_async_copy(source, target, sem)
    copy.start()
    return copy


def add_rows(where, grads, arrived, cuts, after=()):
    block, cols = arrived.shape

    def kernel(where_ref, g_ref, a_ref, *rest):
        outs = rest[len(after) :]
        first = pl.multiple_of(where_ref[0] * block, block)
        for (at, n), out in zip(cuts, outs):
            rows = pl.ds(pl.multiple_of(first + at, 16), n)
            out[...] = g_ref[rows, :].astype(F32) + a_ref[at : at + n, :]

    return pl.pallas_call(
        kernel,
        out_shape=[jax.ShapeDtypeStruct((count, cols), F32) for _, count in cuts],
        in_specs=[SMEM, VMEM, VMEM] + [ANYWHERE] * len(after),
        out_specs=[VMEM] * len(cuts),
        compiler_params=params(),
        cost_estimate=NO_COST,
        name="add_rows",
    )(where, grads, arrived, *after)


def left_terms(me, grads, q_factor, n_shard):
    rows, cols = grads.shape
    block = rows // n_shard
    rank = q_factor.shape[0]
    half = n_shard // 2
    parts = spans(cols, 2 * WIDE)
    out = jax.ShapeDtypeStruct((half * rank, block), F32)

    def kernel(me_ref, g_ref, q_ref, send_ref, keep_ref, qt_ref, *rest):
        wide_refs, acc = rest[:half], rest[half]
        mm = ((1,), (0,))
        for k, (at, n) in enumerate(parts):
            c = slice(at, at + n)
            q3 = pieces(q_ref[:, c]).astype(F32)
            padded = jnp.concatenate([q3, jnp.zeros((LANES - 3 * rank, n), F32)], axis=0)
            q = padded.T.astype(BF16)
            qt_ref[c, :] = q
            value = dot(g_ref[:, c], q, mm)
            acc[...] = value if k == 0 else acc[...] + value
            for d, wide_ref in enumerate(wide_refs):
                first = pl.multiple_of((me_ref[0] ^ (2 * d + 1)) * block, block)
                wide_ref[:, c] = g_ref[pl.ds(first, block), c].astype(F32)
        core = me_ref[0] & 1
        for k in range(half):
            for ref, owner in ((send_ref, 1 - core), (keep_ref, core)):
                first = pl.multiple_of((2 * k + owner) * block, block)
                term = acc[pl.ds(first, block), :].T
                ref[k * rank : (k + 1) * rank, :] = fold(term[: 3 * rank], rank)

    return pl.pallas_call(
        kernel,
        out_shape=[out, out, jax.ShapeDtypeStruct((cols, LANES), BF16)]
        + [jax.ShapeDtypeStruct((block, cols), F32)] * half,
        in_specs=[SMEM, VMEM, VMEM],
        out_specs=[VMEM] * (3 + half),
        scratch_shapes=[pltpu.VMEM((rows, LANES), F32)],
        compiler_params=params(),
        cost_estimate=NO_COST,
        name="left_terms",
    )(me, grads, q_factor)


def error_term(me, error, q_columns, shape, rank):
    block, cols = error.shape
    parts = spans(cols, 2 * WIDE)

    def kernel(me_ref, e_ref, q_ref, out_ref):
        mm = ((1,), (0,))
        value = jnp.zeros((block, LANES), F32)
        for at, n in parts:
            e = e_ref[:, at : at + n]
            q = q_ref[at : at + n, :]
            high = e.astype(BF16)
            mid = (e - high.astype(F32)).astype(BF16)
            value = value + (dot(high, q, mm) + dot(mid, q, mm))
        term = fold(value.T[: 3 * rank], rank)
        for k in range(shape[0] // rank):
            mine = me_ref[0] // 2 == k
            out_ref[k * rank : (k + 1) * rank, :] = jnp.where(mine, term, 0.0)

    return pl.pallas_call(
        kernel,
        out_shape=jax.ShapeDtypeStruct(shape, F32),
        in_specs=[SMEM, VMEM, VMEM],
        out_specs=VMEM,
        compiler_params=params(),
        cost_estimate=NO_COST,
        name="error_term",
    )(me, error, q_columns)


def right_terms(me, grads, error, halves, rank, n_shard, after):
    rows, cols = grads.shape
    block = rows // n_shard
    per = WIDE // LANES
    parts = spans(cols, WIDE)
    n_half = -(-len(parts) // 2)
    out = jax.ShapeDtypeStruct((n_half * per * rank, LANES), F32)

    def kernel(me_ref, g_ref, e_ref, own_ref, other_ref, *rest):
        send_ref, keep_ref, f_all = rest[len(after) :]
        join(me_ref, own_ref, other_ref, f_all)
        f3 = pieces(jnp.concatenate([f_all[j] for j in range(n_shard)], axis=1))
        own = pieces(f_all[me_ref[0]])
        f_own = jnp.concatenate([own, own], axis=1)
        core = me_ref[0] & 1
        mm = ((1,), (0,))
        for k, (at, n) in enumerate(parts):
            c = slice(at, at + n)
            e = e_ref[:, c]
            high = e.astype(BF16)
            mid = (e - high.astype(F32)).astype(BF16)
            value = dot(f3, g_ref[:, c], mm)
            value += dot(f_own, jnp.concatenate([high, mid], axis=0), mm)
            value = fold(value, rank)
            if n < WIDE:
                value = jnp.concatenate([value, jnp.zeros((rank, WIDE - n), F32)], axis=1)
            stacked = jnp.concatenate(
                [value[:, b * LANES : (b + 1) * LANES] for b in range(per)], axis=0
            )
            at_rows = slice((k % n_half) * per * rank, (k % n_half + 1) * per * rank)

            @pl.when(core == k // n_half)
            def _(stacked=stacked, at_rows=at_rows):
                keep_ref[at_rows, :] = stacked

            @pl.when(core != k // n_half)
            def _(stacked=stacked, at_rows=at_rows):
                send_ref[at_rows, :] = stacked

    return pl.pallas_call(
        kernel,
        out_shape=[out, out],
        in_specs=[SMEM, VMEM, VMEM, VMEM, VMEM] + [ANYWHERE] * len(after),
        out_specs=[VMEM, VMEM],
        scratch_shapes=[pltpu.VMEM((n_shard, rank, block), F32)],
        compiler_params=params(),
        cost_estimate=NO_COST,
        name="right_terms",
    )(me, grads, error, *halves, *after)


def finish(core, both, q_own, q_other, partial, arrived):
    rows, cols = partial.shape
    rank = both.shape[0] - rows
    per = WIDE // LANES
    parts = spans(cols, WIDE)
    row_parts = spans(rows, 32)
    n_half = q_own.shape[0] // (per * rank)
    counts = [a.shape[0] for a in arrived]
    n_arrived = len(arrived)

    def kernel(core_ref, both_ref, own_ref, other_ref, p_ref, *rest):
        a_refs = rest[:n_arrived]
        approx_ref, error_ref, q_ref, o_buf, n_buf, q_buf, sems = rest[n_arrived:]
        out = []
        left = both_ref[...]
        for k, (at, n) in enumerate(parts):
            c = slice(at, at + n)
            at_rows = slice((k % n_half) * per * rank, (k % n_half + 1) * per * rank)
            mine = core_ref[0] == k // n_half
            stacked = jnp.where(mine, own_ref[at_rows, :], other_ref[at_rows, :])
            q_sum = jnp.concatenate(
                [stacked[b * rank : (b + 1) * rank] for b in range(n // LANES)], axis=1
            )
            value = dot(left, six(q_sum, 0, False), ((1,), (0,)))
            q_buf[:, c] = value[:rank]
            o_buf[:, c] = value[rank:]
        out.append(started(q_buf, q_ref, sems.at[0, 0]))
        for k, (at, n) in enumerate(row_parts):
            r = pl.ds(at, n)
            out.append(started(o_buf.at[r, :], approx_ref.at[r, :], sems.at[1, k]))
        first = 0
        for count, a_ref in zip(counts, a_refs):
            for at, n in spans(count, 16):
                r = slice(first + at, first + at + n)
                n_buf[r, :] = (p_ref[r, :] + a_ref[at : at + n, :]) - o_buf[r, :]
                rows_out = pl.ds(first + at, n)
                k = (first + at) // 16
                out.append(started(n_buf.at[rows_out, :], error_ref.at[rows_out, :], sems.at[2, k]))
            first += count
        for copy in out:
            copy.wait()

    return pl.pallas_call(
        kernel,
        out_shape=[
            jax.ShapeDtypeStruct((rows, cols), F32),
            jax.ShapeDtypeStruct((rows, cols), F32),
            jax.ShapeDtypeStruct((rank, cols), F32),
        ],
        in_specs=[SMEM] + [VMEM] * (4 + n_arrived),
        out_specs=[ANYWHERE] * 3,
        scratch_shapes=[pltpu.VMEM((rows, cols), F32)] * 2
        + [
            pltpu.VMEM((rank, cols), F32),
            pltpu.SemaphoreType.DMA((3, -(-rows // 16))),
        ],
        compiler_params=params(),
        cost_estimate=NO_COST,
        name="finish",
    )(core, both, q_own, q_other, partial, *arrived)


def inverse_factor(me, halves, rank, n_rep, n_shard, after):
    block = halves[0].shape[1]

    def kernel(me_ref, own_ref, other_ref, *rest):
        both_ref, f_all = rest[-2:]
        join(me_ref, own_ref, other_ref, f_all)
        f = jnp.concatenate([f_all[j] for j in range(n_shard)], axis=1)
        gram = dot(f, f, ((1,), (1,)), lax.Precision.HIGHEST)
        row = lax.broadcasted_iota(jnp.int32, (rank, 2 * rank), 0)
        col = lax.broadcasted_iota(jnp.int32, (rank, 2 * rank), 1)
        unit = jnp.where(col == row + rank, 1.0, 0.0).astype(F32)
        w = jnp.concatenate([gram, jnp.zeros_like(gram)], axis=1) + unit
        for k in range(rank):
            column = w[:, k : k + 1] * (1.0 / w[k : k + 1, k : k + 1])
            w = jnp.where(row > k, w - column * w[k : k + 1, :], w)
        pivots = jnp.sum(jnp.where(row == col, w, 0.0), axis=1, keepdims=True)
        w = w * (1.0 / jnp.sqrt(pivots))
        inverse = w[:, rank:]
        basis = dot(inverse, f_all[me_ref[0]], ((1,), (0,)), lax.Precision.HIGHEST)
        to_approx = dot(basis.T, inverse, ((1,), (0,)), lax.Precision.HIGHEST)
        both = jnp.concatenate([inverse, to_approx], axis=0) * (1.0 / n_rep)
        both_ref[...] = six(both, 1, True)

    return pl.pallas_call(
        kernel,
        out_shape=jax.ShapeDtypeStruct((rank + block, 6 * rank), BF16),
        in_specs=[SMEM, VMEM, VMEM] + [ANYWHERE] * len(after),
        out_specs=VMEM,
        scratch_shapes=[pltpu.VMEM((n_shard, rank, block), F32)],
        compiler_params=params(),
        cost_estimate=NO_COST,
        name="inverse_factor",
    )(me, *halves, *after)


def group_sum(value, axes, first, bits, after=()):
    moved = [partner(value, axes, d << first) for d in range(1, 1 << bits)]
    return total([value, *moved], after)


def pair_sum(value, axes, bit, after=()):
    return total([value, partner(value, axes, 1 << bit)], after)


def body(grads, error, q_factor):
    n_rep, n_y = lax.axis_size("rep"), lax.axis_size("y")
    n_shard = 2 * n_y
    grads, error = grads[0, 0], error[0]
    rows, cols = grads.shape
    block = rows // n_shard
    rank = q_factor.shape[0]
    core = lax.axis_index("core").astype(jnp.int32)
    here = 2 * lax.axis_index("y").astype(jnp.int32) + core
    me, core = here.reshape(1), core.reshape(1)
    chips = ("rep", "y")
    n_bits = (n_rep * n_y).bit_length() - 1
    distances = range(1, n_y)
    cuts = [(0, 80), (80, block - 80)]

    send, keep, q_columns, own_wide, *wide = left_terms(me, grads, q_factor, n_shard)
    from_other = partner(send, "core", 1)
    half = total([keep, from_other, error_term(me, error, q_columns, keep.shape, rank)])
    sums = [
        add_rows(me ^ (2 * d), grads, partner(passed_on(w, [half]), "core", 1), cuts)
        for d, w in zip(distances, wide)
    ]

    def over_y(k, after=None):
        values = [value[k] for value in sums]
        if after is not None:
            values = [passed_on(value, after) for value in values]
        moved = [partner(value, "y", d) for d, value in zip(distances, values)]
        return values, moved[0] if n_y == 2 else sum(moved)

    half = pair_sum(half, chips, 0)
    crossing, first_part = over_y(0, [half])
    from_core = partner(passed_on(own_wide, [half]), "core", 1)
    half = pair_sum(half, chips, 1, [value[0] for value in sums])
    half = group_sum(half, chips, 2, n_bits - 2, crossing)
    halves = [half, partner(half, "core", 1)]

    send, keep = right_terms(me, grads, error, halves, rank, n_shard, [from_core])
    both = inverse_factor(me, halves, rank, n_rep, n_shard, [send])
    own_half = total([keep, partner(send, "core", 1)], [both])
    parts = exchange(own_half.reshape(n_rep, -1, LANES), "rep")
    piece = sum_parts(parts, [first_part])
    values, second_part = over_y(1, [piece])
    piece = [piece] + [partner(piece, "y", d) for d in distances]
    pieces_out = total(piece, values, n_rep)
    own_terms = lax.dynamic_slice(grads, (here * block, 0), (block, cols)).astype(F32)
    partial = (own_terms + from_core) + error
    q_own = exchange(pieces_out, "rep").reshape(own_half.shape)
    q_own = passed_on(q_own, [partial])
    q_other = partner(q_own, "core", 1)

    arrived = [first_part, second_part]
    approx, new_error, q_next = finish(core, both, q_own, q_other, partial, arrived)
    return approx, new_error[None], q_next


def solution(mesh):
    n_rep, n_shard = mesh.devices.shape
    mesh = Mesh(mesh.devices.reshape(n_rep, n_shard // 2, 2), ("rep", "y", "core"))
    shard = ("y", "core")
    in_specs = (P("rep", shard, None, None), P("rep", shard, None), P())
    out_specs = (P(shard, None), P("rep", shard, None), P())
    return jax.shard_map(body, mesh=mesh, in_specs=in_specs, out_specs=out_specs, check_vma=False)
```

```python
import jax
import jax.numpy as jnp
from jax import lax
from jax.experimental import pallas as pl
from jax.experimental.pallas import tpu as pltpu
from jax.sharding import Mesh, PartitionSpec as P

F32 = jnp.float32
BF16 = jnp.bfloat16
LANES = 128
WIDE = 512
VMEM_LIMIT = 24 * 1024 * 1024


def pieces(x):
    high = x.astype(BF16)
    rest = x - high.astype(F32)
    mid = rest.astype(BF16)
    low = (rest - mid.astype(F32)).astype(BF16)
    return jnp.concatenate([high, mid, low], axis=0)


def fold(x, rank):
    return (x[2 * rank :] + x[rank : 2 * rank]) + x[:rank]


def dot(a, b, contract, precision=None):
    return lax.dot_general(
        a, b, (contract, ((), ())), precision=precision, preferred_element_type=F32
    )


def six(x, axis, left):
    high = x.astype(BF16)
    rest = x - high.astype(F32)
    mid = rest.astype(BF16)
    low = (rest - mid.astype(F32)).astype(BF16)
    order = [high, high, mid, high, low, mid] if left else [high, mid, high, low, high, mid]
    return jnp.concatenate(order, axis=axis)


def params(limit=VMEM_LIMIT):
    return pltpu.CompilerParams(vmem_limit_bytes=limit)


NO_COST = pl.CostEstimate(flops=0, bytes_accessed=0, transcendentals=0)


def partner(x, axis, d):
    return lax.ppermute(x, axis, [(i, i ^ d) for i in range(lax.axis_size(axis))])


def whole(shape):
    return pl.BlockSpec(shape, lambda *_: (0,) * len(shape))


ANYWHERE = pl.BlockSpec(memory_space=pl.ANY)
VMEM = pl.BlockSpec(memory_space=pltpu.VMEM)
SMEM = pl.BlockSpec(memory_space=pltpu.SMEM)


def exchange(parts, axes):
    return lax.all_to_all(parts, axes, split_axis=0, concat_axis=0, tiled=True)


def tree(values):
    values = list(values)
    while len(values) > 1:
        values = [sum(values[i + 1 : i + 2], values[i]) for i in range(0, len(values), 2)]
    return values[0]


def total(values, after=(), repeat=None):
    n = len(values)
    shape = values[0].shape

    def kernel(*refs):
        value = tree([r[...] for r in refs[:n]])
        if repeat is None:
            refs[-1][...] = value
        else:
            for k in range(repeat):
                refs[-1][k] = value

    return pl.pallas_call(
        kernel,
        out_shape=jax.ShapeDtypeStruct(shape if repeat is None else (repeat, *shape), F32),
        in_specs=[VMEM] * n + [ANYWHERE] * len(after),
        out_specs=VMEM,
        compiler_params=params(),
        cost_estimate=NO_COST,
        name="total",
    )(*values, *after)


def sum_parts(parts, after=()):
    n = parts.shape[0]

    def kernel(p_ref, *rest):
        rest[-1][...] = tree([p_ref[k] for k in range(n)])

    return pl.pallas_call(
        kernel,
        out_shape=jax.ShapeDtypeStruct(parts.shape[1:], F32),
        in_specs=[VMEM] + [ANYWHERE] * len(after),
        out_specs=VMEM,
        compiler_params=params(),
        cost_estimate=NO_COST,
        name="sum_parts",
    )(parts, *after)


def passed_on(value, after):
    def kernel(*refs):
        pass

    return pl.pallas_call(
        kernel,
        out_shape=jax.ShapeDtypeStruct(value.shape, value.dtype),
        in_specs=[ANYWHERE] * (1 + len(after)),
        out_specs=ANYWHERE,
        input_output_aliases={0: 0},
        compiler_params=params(),
        cost_estimate=NO_COST,
        name="passed_on",
    )(value, *after)


def join(me_ref, own_ref, other_ref, f_all):
    n_shard, rank, _ = f_all.shape
    half = n_shard // 2
    core = me_ref[0] & 1
    for k in range(half):
        f_all[2 * k + core] = own_ref[k * rank : (k + 1) * rank]
        f_all[2 * k + 1 - core] = other_ref[k * rank : (k + 1) * rank]


def spans(size, step):
    return [(at, min(step, size - at)) for at in range(0, size, step)]


def started(source, target, sem):
    copy = pltpu.make_async_copy(source, target, sem)
    copy.start()
    return copy


def add_rows(where, grads, arrived, cuts, after=()):
    block, cols = arrived.shape

    def kernel(where_ref, g_ref, a_ref, *rest):
        outs = rest[len(after) :]
        first = pl.multiple_of(where_ref[0] * block, block)
        for col, width in spans(cols, WIDE):
            c = slice(col, col + width)
            value = g_ref[pl.ds(first, block), c].astype(F32)
            for (at, n), out in zip(cuts, outs):
                out[:, c] = value[at : at + n] + a_ref[at : at + n, c]

    return pl.pallas_call(
        kernel,
        out_shape=[jax.ShapeDtypeStruct((count, cols), F32) for _, count in cuts],
        in_specs=[SMEM, VMEM, VMEM] + [ANYWHERE] * len(after),
        out_specs=[VMEM] * len(cuts),
        compiler_params=params(),
        cost_estimate=NO_COST,
        name="add_rows",
    )(where, grads, arrived, *after)


def left_terms(me, grads, q_factor, n_shard):
    rows, cols = grads.shape
    block = rows // n_shard
    rank = q_factor.shape[0]
    half = n_shard // 2
    parts = spans(cols, 2 * WIDE)
    out = jax.ShapeDtypeStruct((half * rank, block), F32)

    def kernel(me_ref, g_ref, q_ref, send_ref, keep_ref, qt_ref, *rest):
        wide_refs, acc = rest[:half], rest[half]
        mm = ((1,), (0,))
        for k, (at, n) in enumerate(parts):
            c = slice(at, at + n)
            q3 = pieces(q_ref[:, c]).astype(F32)
            padded = jnp.concatenate([q3, jnp.zeros((LANES - 3 * rank, n), F32)], axis=0)
            q = padded.T.astype(BF16)
            qt_ref[c, :] = q
            value = dot(g_ref[:, c], q, mm)
            acc[...] = value if k == 0 else acc[...] + value
            for d, wide_ref in enumerate(wide_refs):
                first = pl.multiple_of((me_ref[0] ^ (2 * d + 1)) * block, block)
                wide_ref[:, c] = g_ref[pl.ds(first, block), c].astype(F32)
        core = me_ref[0] & 1
        for k in range(half):
            for ref, owner in ((send_ref, 1 - core), (keep_ref, core)):
                first = pl.multiple_of((2 * k + owner) * block, block)
                term = acc[pl.ds(first, block), :].T
                ref[k * rank : (k + 1) * rank, :] = fold(term[: 3 * rank], rank)

    return pl.pallas_call(
        kernel,
        out_shape=[out, out, jax.ShapeDtypeStruct((cols, LANES), BF16)]
        + [jax.ShapeDtypeStruct((block, cols), F32)] * half,
        in_specs=[SMEM, VMEM, VMEM],
        out_specs=[VMEM] * (3 + half),
        scratch_shapes=[pltpu.VMEM((rows, LANES), F32)],
        compiler_params=params(),
        cost_estimate=NO_COST,
        name="left_terms",
    )(me, grads, q_factor)


def error_term(me, error, q_columns, shape, rank):
    block, cols = error.shape
    parts = spans(cols, 2 * WIDE)

    def kernel(me_ref, e_ref, q_ref, out_ref):
        mm = ((1,), (0,))
        value = jnp.zeros((block, LANES), F32)
        for at, n in parts:
            e = e_ref[:, at : at + n]
            q = q_ref[at : at + n, :]
            high = e.astype(BF16)
            mid = (e - high.astype(F32)).astype(BF16)
            value = value + (dot(high, q, mm) + dot(mid, q, mm))
        term = fold(value.T[: 3 * rank], rank)
        for k in range(shape[0] // rank):
            mine = me_ref[0] // 2 == k
            out_ref[k * rank : (k + 1) * rank, :] = jnp.where(mine, term, 0.0)

    return pl.pallas_call(
        kernel,
        out_shape=jax.ShapeDtypeStruct(shape, F32),
        in_specs=[SMEM, VMEM, VMEM],
        out_specs=VMEM,
        compiler_params=params(),
        cost_estimate=NO_COST,
        name="error_term",
    )(me, error, q_columns)


def right_terms(me, grads, error, halves, rank, n_shard, after):
    rows, cols = grads.shape
    block = rows // n_shard
    per = WIDE // LANES
    parts = spans(cols, WIDE)
    n_half = -(-len(parts) // 2)
    out = jax.ShapeDtypeStruct((n_half * per * rank, LANES), F32)

    def kernel(me_ref, g_ref, e_ref, own_ref, other_ref, *rest):
        send_ref, keep_ref, f_all = rest[len(after) :]
        join(me_ref, own_ref, other_ref, f_all)
        f3 = pieces(jnp.concatenate([f_all[j] for j in range(n_shard)], axis=1))
        own = pieces(f_all[me_ref[0]])
        f_own = jnp.concatenate([own, own], axis=1)
        core = me_ref[0] & 1
        mm = ((1,), (0,))
        for k, (at, n) in enumerate(parts):
            c = slice(at, at + n)
            e = e_ref[:, c]
            high = e.astype(BF16)
            mid = (e - high.astype(F32)).astype(BF16)
            value = dot(f3, g_ref[:, c], mm)
            value += dot(f_own, jnp.concatenate([high, mid], axis=0), mm)
            value = fold(value, rank)
            if n < WIDE:
                value = jnp.concatenate([value, jnp.zeros((rank, WIDE - n), F32)], axis=1)
            stacked = jnp.concatenate(
                [value[:, b * LANES : (b + 1) * LANES] for b in range(per)], axis=0
            )
            at_rows = slice((k % n_half) * per * rank, (k % n_half + 1) * per * rank)

            @pl.when(core == k // n_half)
            def _(stacked=stacked, at_rows=at_rows):
                keep_ref[at_rows, :] = stacked

            @pl.when(core != k // n_half)
            def _(stacked=stacked, at_rows=at_rows):
                send_ref[at_rows, :] = stacked

    return pl.pallas_call(
        kernel,
        out_shape=[out, out],
        in_specs=[SMEM, VMEM, VMEM, VMEM, VMEM] + [ANYWHERE] * len(after),
        out_specs=[VMEM, VMEM],
        scratch_shapes=[pltpu.VMEM((n_shard, rank, block), F32)],
        compiler_params=params(),
        cost_estimate=NO_COST,
        name="right_terms",
    )(me, grads, error, *halves, *after)


def finish(core, both, q_own, q_other, partial, arrived):
    rows, cols = partial.shape
    rank = both.shape[0] - rows
    per = WIDE // LANES
    parts = spans(cols, WIDE)
    n_half = q_own.shape[0] // (per * rank)
    counts = [a.shape[0] for a in arrived]
    n_arrived = len(arrived)

    def kernel(core_ref, both_ref, own_ref, other_ref, p_ref, *rest):
        a_refs = rest[:n_arrived]
        approx_ref, error_ref, q_ref, o_buf, n_buf, q_buf, sems = rest[n_arrived:]
        out = []
        left = both_ref[...]

        def product(k):
            n = parts[k][1]
            at_rows = slice((k % n_half) * per * rank, (k % n_half + 1) * per * rank)
            mine = core_ref[0] == k // n_half
            stacked = jnp.where(mine, own_ref[at_rows, :], other_ref[at_rows, :])
            q_sum = jnp.concatenate(
                [stacked[b * rank : (b + 1) * rank] for b in range(n // LANES)], axis=1
            )
            return dot(left, six(q_sum, 0, False), ((1,), (0,)))

        later = product(0)
        for k, (at, n) in enumerate(parts):
            value = later
            if k + 1 < len(parts):
                later = product(k + 1)
            c = slice(at, at + n)
            q_buf[:, c] = value[:rank]
            o_buf[:, c] = value[rank:]
            first = 0
            for count, a_ref in zip(counts, a_refs):
                r = slice(first, first + count)
                n_buf[r, c] = (p_ref[r, c] + a_ref[:, c]) - value[rank + first : rank + first + count]
                first += count
            for i, (buf, ref) in enumerate(
                ((o_buf, approx_ref), (n_buf, error_ref), (q_buf, q_ref))
            ):
                out.append(
                    started(buf.at[:, pl.ds(at, n)], ref.at[:, pl.ds(at, n)], sems.at[i, k])
                )
        for copy in out:
            copy.wait()

    return pl.pallas_call(
        kernel,
        out_shape=[
            jax.ShapeDtypeStruct((rows, cols), F32),
            jax.ShapeDtypeStruct((rows, cols), F32),
            jax.ShapeDtypeStruct((rank, cols), F32),
        ],
        in_specs=[SMEM] + [VMEM] * (4 + n_arrived),
        out_specs=[ANYWHERE] * 3,
        scratch_shapes=[pltpu.VMEM((rows, cols), F32)] * 2
        + [
            pltpu.VMEM((rank, cols), F32),
            pltpu.SemaphoreType.DMA((3, len(parts))),
        ],
        compiler_params=params(),
        cost_estimate=NO_COST,
        name="finish",
    )(core, both, q_own, q_other, partial, *arrived)


def inverse_factor(me, halves, rank, n_rep, n_shard, after):
    block = halves[0].shape[1]

    def kernel(me_ref, own_ref, other_ref, *rest):
        both_ref, f_all = rest[-2:]
        join(me_ref, own_ref, other_ref, f_all)
        f = jnp.concatenate([f_all[j] for j in range(n_shard)], axis=1)
        gram = dot(f, f, ((1,), (1,)), lax.Precision.HIGHEST)
        row = lax.broadcasted_iota(jnp.int32, (rank, 2 * rank), 0)
        col = lax.broadcasted_iota(jnp.int32, (rank, 2 * rank), 1)
        unit = jnp.where(col == row + rank, 1.0, 0.0).astype(F32)
        w = jnp.concatenate([gram, jnp.zeros_like(gram)], axis=1) + unit
        for k in range(rank):
            scale = 1.0 / jnp.sqrt(w[k : k + 1, k : k + 1])
            pivot = w[k : k + 1, :] * scale
            column = w[:, k : k + 1] * scale
            w = jnp.where(row > k, w - column * pivot, jnp.where(row == k, pivot, w))
        inverse = w[:, rank:]
        basis = dot(inverse, f_all[me_ref[0]], ((1,), (0,)), lax.Precision.HIGHEST)
        to_approx = dot(basis.T, inverse, ((1,), (0,)), lax.Precision.HIGHEST)
        both = jnp.concatenate([inverse, to_approx], axis=0) * (1.0 / n_rep)
        both_ref[...] = six(both, 1, True)

    return pl.pallas_call(
        kernel,
        out_shape=jax.ShapeDtypeStruct((rank + block, 6 * rank), BF16),
        in_specs=[SMEM, VMEM, VMEM] + [ANYWHERE] * len(after),
        out_specs=VMEM,
        scratch_shapes=[pltpu.VMEM((n_shard, rank, block), F32)],
        compiler_params=params(),
        cost_estimate=pl.CostEstimate(flops=0, bytes_accessed=1 << 24, transcendentals=0),
        name="inverse_factor",
    )(me, *halves, *after)


def group_sum(value, axes, first, bits, after=()):
    moved = [partner(value, axes, d << first) for d in range(1, 1 << bits)]
    return total([value, *moved], after)


def pair_sum(value, axes, bit, after=()):
    return total([value, partner(value, axes, 1 << bit)], after)


def body(grads, error, q_factor):
    n_rep, n_y = lax.axis_size("rep"), lax.axis_size("y")
    n_shard = 2 * n_y
    grads, error = grads[0, 0], error[0]
    rows, cols = grads.shape
    block = rows // n_shard
    rank = q_factor.shape[0]
    core = lax.axis_index("core").astype(jnp.int32)
    here = 2 * lax.axis_index("y").astype(jnp.int32) + core
    me, core = here.reshape(1), core.reshape(1)
    chips = ("rep", "y")
    n_bits = (n_rep * n_y).bit_length() - 1
    distances = range(1, n_y)
    cuts = [(0, 72), (72, block - 72)]

    send, keep, q_columns, own_wide, *wide = left_terms(me, grads, q_factor, n_shard)
    from_other = partner(send, "core", 1)
    half = total([keep, from_other, error_term(me, error, q_columns, keep.shape, rank)])
    sums = [
        add_rows(me ^ (2 * d), grads, partner(passed_on(w, [half]), "core", 1), cuts)
        for d, w in zip(distances, wide)
    ]

    def over_y(k, after=None):
        values = [value[k] for value in sums]
        if after is not None:
            values = [passed_on(value, after) for value in values]
        moved = [partner(value, "y", d) for d, value in zip(distances, values)]
        return values, moved[0] if n_y == 2 else sum(moved)

    half = pair_sum(half, chips, 0)
    crossing, first_part = over_y(0, [half])
    from_core = partner(passed_on(own_wide, [half]), "core", 1)
    half = pair_sum(half, chips, 1, [value[0] for value in sums])
    half = group_sum(half, chips, 2, n_bits - 2, crossing)
    halves = [half, partner(half, "core", 1)]

    send, keep = right_terms(me, grads, error, halves, rank, n_shard, [from_core])
    own_half = total([keep, partner(send, "core", 1)])
    both = inverse_factor(me, halves, rank, n_rep, n_shard, [own_half])
    parts = exchange(own_half.reshape(n_rep, -1, LANES), "rep")
    piece = sum_parts(parts, [first_part, both])
    values, second_part = over_y(1, [piece])
    piece = [piece] + [partner(piece, "y", d) for d in distances]
    pieces_out = total(piece, values, n_rep)
    own_terms = lax.dynamic_slice(grads, (here * block, 0), (block, cols)).astype(F32)
    partial = (own_terms + from_core) + error
    q_own = exchange(pieces_out, "rep").reshape(own_half.shape)
    q_own = passed_on(q_own, [partial])
    q_other = partner(q_own, "core", 1)

    arrived = [first_part, second_part]
    approx, new_error, q_next = finish(core, both, q_own, q_other, partial, arrived)
    return approx, new_error[None], q_next


def solution(mesh):
    n_rep, n_shard = mesh.devices.shape
    mesh = Mesh(mesh.devices.reshape(n_rep, n_shard // 2, 2), ("rep", "y", "core"))
    shard = ("y", "core")
    in_specs = (P("rep", shard, None, None), P("rep", shard, None), P())
    out_specs = (P(shard, None), P("rep", shard, None), P())
    return jax.shard_map(body, mesh=mesh, in_specs=in_specs, out_specs=out_specs, check_vma=False)
```
